32 devices in a mesh: rows: 8 (over z, y), cols: 4 (over x, core).
Axes of the slice: x: 2, y: 2, z: 4, core: 2. Of those that a mesh axis runs over, the one named last changes fastest.
Arguments:
- features: bfloat16 [8192, 256], P(('rows', 'cols')), may hold values from -6 to 6
- weight: bfloat16 [256, 256], replicated, may hold values from -0.375 to 0.375
- bias: float32 [256], replicated, may hold values from -3 to 3
- tile_values: bfloat16 [8, 4, 8, 3, 128, 128], P('rows', 'cols'), may hold values from -0.21875 to 0.21875
- tile_source: int32 [8, 4, 8, 3], P('rows', 'cols'), may hold values from 0 to 7
- tile_dest: int32 [8, 4, 8, 3], P('rows', 'cols'), may hold values from 0 to 1
- send_counts: int32 [8, 4, 8], P('rows', 'cols'), may hold values from 0 to 3, as said below
- cotangent: bfloat16 [8192, 256], P(('rows', 'cols')), may hold values from -6 to 6
Outputs:
- output: bfloat16 [8192, 256], P(('rows', 'cols'))
- input_grad: bfloat16 [8192, 256], P(('rows', 'cols'))
- weight_grad: float32 [256, 256], replicated
- bias_grad: float32 [256], replicated
The draws below stay inside these ranges and needn't reach their ends.
Inputs may be any that keep to these rules, and one draw needn't show every extreme that they name: `send_counts`: in each column group one owner, drawn from the seed, receives 3 live slots from every sender.
All inputs are finite; a program needn't handle non-finite values.
Results may differ from the reference program's by a relative error of at most 0.014.
Values may be sent and summed in bfloat16 or wider, within the bound.
No kernel may reach another device: no remote copies, remote signals or barrier semaphores. Data moves between devices by JAX's collectives and lax.ppermute only.
A program may use at most 128 MiB of HBM per device.

```python
import jax
import jax.numpy as jnp
from jax import lax

F = 256
TILE = 128
TD = 2
CAP = 3
NODES = 8192
N_ROWS = 8
N_COLS = 4


def draw_send_counts(key, part):
    key_base, key_full = jax.random.split(jax.random.fold_in(key, 17))
    base_counts = jax.random.randint(key_base, (N_ROWS, N_COLS, N_ROWS), 0, CAP + 1)
    full_owner = jax.random.randint(key_full, (N_COLS,), 0, N_ROWS)
    owner_hit = full_owner[None, :, None] == jnp.arange(N_ROWS)[None, None, :]
    return jnp.where(owner_hit, CAP, base_counts).astype(jnp.int32)


def plant(drawn, own_key, smallest, largest):
    shape = drawn.shape
    index_at = [jax.random.randint(jax.random.fold_in(own_key, axis), (), 0, shape[axis]) for axis in range(len(shape))]
    drawn = drawn.at[tuple(index_at)].set(smallest)
    longest = shape.index(max(shape))
    index_at[longest] = (index_at[longest] + 1) % shape[longest]
    return drawn.at[tuple(index_at)].set(largest)


def steps_of(rng, dims, cuts, smallest, top_value):
    gain, own = 1.0, jax.random.fold_in(rng, 6)
    for position, parts in cuts:
        steps = jnp.exp(jax.random.uniform(jax.random.fold_in(own, position), (parts,), jnp.float32, smallest / len(cuts), top_value / len(cuts)))
        gain = gain * jnp.repeat(steps, dims[position] // parts).reshape([-1 if axis == position else 1 for axis in range(len(dims))])
    return gain


def scatter_about(own_key, dims, scale, limit, shards=(), kind=jnp.bfloat16):
    values = scale * jax.random.normal(own_key, dims, jnp.float32)
    if shards:
        values = values * steps_of(own_key, dims, shards, -0.22, 0.18)
    return jnp.clip(values, -limit, limit).astype(kind)


def setup_inputs(seed: int = 0) -> dict:
    splits = jax.random.split(jax.random.key(seed), 9)
    features = scatter_about(splits[0], (NODES, F), 1.0, 6.0, ((0, 32),))
    weight = scatter_about(splits[1], (F, F), F ** -0.5, 0.375)
    bias = scatter_about(splits[2], (F,), 0.5, 3.0, (), jnp.float32)
    tile_values = scatter_about(splits[3], (N_ROWS, N_COLS, N_ROWS, CAP, TILE, TILE), (TILE * N_ROWS * CAP // (2 * TD)) ** -0.5, 0.21875, ((0, 8), (1, 4)))
    tile_source = plant(jax.random.randint(splits[4], (N_ROWS, N_COLS, N_ROWS, CAP), 0, N_COLS * TD), jax.random.fold_in(splits[4], 1), 0, (N_COLS * TD) - 1).astype(jnp.int32)
    tile_dest = plant(jax.random.randint(splits[5], (N_ROWS, N_COLS, N_ROWS, CAP), 0, TD), jax.random.fold_in(splits[5], 1), 0, TD - 1).astype(jnp.int32)
    send_counts = draw_send_counts(jax.random.fold_in(splits[8], 71), 0)
    cotangent = scatter_about(splits[7], (NODES, F), 1.0, 6.0, ((0, 32),))
    return dict(features=features, weight=weight, bias=bias, tile_values=tile_values, tile_source=tile_source, tile_dest=tile_dest, send_counts=send_counts, cotangent=cotangent)


def reference(features, weight, bias, tile_values, tile_source, tile_dest, send_counts, cotangent):
    width = weight.shape[1]
    hidden = jnp.dot(features, weight, preferred_element_type=jnp.float32).astype(jnp.bfloat16)
    block_tiles = hidden.reshape(N_ROWS, N_COLS * TD, TILE, width)
    slot_ids = jnp.arange(CAP, dtype=jnp.int32)
    dest_ids = jnp.arange(TD, dtype=jnp.int32)
    span_ids = jnp.arange(N_COLS * TD, dtype=jnp.int32)
    owner_ids = jnp.arange(N_ROWS, dtype=jnp.int32)

    def device_data(device_step):
        row_index = device_step // N_COLS
        col_index = device_step % N_COLS
        live_slots = (slot_ids[None, :] < send_counts[row_index, col_index][:, None]).astype(jnp.float32)
        tile_vals = tile_values[row_index, col_index].astype(jnp.float32)
        return (row_index, col_index, tile_vals, tile_source[row_index, col_index], tile_dest[row_index, col_index], live_slots)

    def push_step(running, device_step):
        row_index, col_index, tile_vals, source_ids, target_ids, live_slots = device_data(device_step)
        chosen = block_tiles[row_index][source_ids].astype(jnp.float32)
        partial_tiles = jnp.einsum('osab,osaf->osbf', tile_vals, chosen)
        routing = (target_ids[:, :, None] == dest_ids[None, None, :]).astype(jnp.float32) * live_slots[:, :, None]
        contrib = jnp.einsum('ost,osbf->otbf', routing, partial_tiles).astype(jnp.bfloat16)
        return (running.at[:, col_index].add(contrib.astype(jnp.float32)), None)
    steps_all = jnp.arange(N_ROWS * N_COLS, dtype=jnp.int32)
    start_sum = jnp.zeros((N_ROWS, N_COLS, TD, TILE, width), jnp.float32)
    summed, _ = lax.scan(push_step, start_sum, steps_all)
    pre = summed.reshape(-1, width) + bias.astype(jnp.float32)[None, :]
    output = jax.nn.gelu(pre).astype(jnp.bfloat16)
    _, backward_fn = jax.vjp(jax.nn.gelu, pre)
    grad_pre = backward_fn(cotangent.astype(jnp.float32))[0].astype(jnp.bfloat16)
    grad_tiles = grad_pre.reshape(N_ROWS, N_COLS, TD, TILE, width)

    def pull_step(running, device_step):
        row_index, col_index, tile_vals, source_ids, target_ids, live_slots = device_data(device_step)
        column_grads = grad_tiles[:, col_index]
        chosen = column_grads[owner_ids[:, None], target_ids].astype(jnp.float32)
        term = jnp.einsum('osab,osbf->osaf', tile_vals, chosen) * live_slots[:, :, None, None]
        spread = (source_ids[:, :, None] == span_ids[None, None, :]).astype(jnp.float32)
        piece_sum = jnp.einsum('osj,osaf->jaf', spread, term)
        return (running.at[row_index].add(piece_sum), None)
    start_grad = jnp.zeros((N_ROWS, N_COLS * TD, TILE, width), jnp.float32)
    grad_sum, _ = lax.scan(pull_step, start_grad, steps_all)
    grad_rounded = grad_sum.reshape(-1, width).astype(jnp.bfloat16)
    input_grad = jnp.dot(grad_rounded, weight.T, preferred_element_type=jnp.float32).astype(jnp.bfloat16)
    scale_factor = 1.0 / jnp.sqrt(jnp.float32(NODES))
    weight_grad = jnp.dot(features.T, grad_rounded, preferred_element_type=jnp.float32) * scale_factor
    bias_grad = lax.optimization_barrier(jnp.sum(grad_pre.astype(jnp.float32), axis=0)) * scale_factor
    return (output, input_grad, weight_grad, bias_grad)
```

```python
import functools
import math

import jax
import jax.numpy as jnp
from jax import lax
from jax.experimental import pallas as pl
from jax.experimental.pallas import tpu as pltpu
from jax.sharding import PartitionSpec as P

F32 = jnp.float32
BF16 = jnp.bfloat16
PAD = 16


def call(body, out_shape, scratch=(), n_smem=0, n_vmem=0, flops=0):
    specs = [pl.BlockSpec(memory_space=pltpu.SMEM)] * n_smem
    specs += [pl.BlockSpec(memory_space=pltpu.VMEM)] * n_vmem
    many = isinstance(out_shape, (list, tuple))
    vmem = pl.BlockSpec(memory_space=pltpu.VMEM)
    return pl.pallas_call(
        body,
        out_shape=out_shape,
        in_specs=specs,
        out_specs=[vmem] * len(out_shape) if many else vmem,
        scratch_shapes=list(scratch),
        cost_estimate=pl.CostEstimate(flops=flops, bytes_accessed=2_000_000, transcendentals=0),
        compiler_params=pltpu.CompilerParams(vmem_limit_bytes=48 * 1024 * 1024),
    )


def tree_sum(items):
    items = [x.astype(F32) for x in items]
    while len(items) > 1:
        items = [items[i] + items[i + 1] for i in range(0, len(items), 2)]
    return items[0]


def send(x, axis, offset):
    size = lax.axis_size(axis)
    return lax.ppermute(x, axis, [(i, i ^ offset) for i in range(size)])


def push_kernel(rows, slots, tiles, span, code_ref, place_ref, *refs):
    feat_refs, vals_ref, out_ref, turned = refs[:-3], refs[-3], refs[-2], refs[-1]
    size = vals_ref.shape[-1]
    row, col = place_ref[0], place_ref[1]
    for k, ref in enumerate(feat_refs):
        for t in range(tiles):
            turned[(col ^ k) * tiles + t] = ref[t * size : (t + 1) * size, :].T
    for k in range(rows):
        owner = row ^ k
        total = None
        for s in range(slots):
            word = code_ref[owner * slots + s]
            vals = vals_ref[owner, s]
            zero = jnp.zeros_like(vals)
            picked = jnp.concatenate(
                [jnp.where(word % 256 == t, vals, zero) for t in range(tiles)], axis=1
            )
            part = jnp.dot(turned[word // 256], picked, preferred_element_type=F32)
            total = part if total is None else total + part
        out_ref[k] = total.astype(BF16)


def middle_kernel(cols, n_parts, place_ref, *refs):
    parts = refs[:n_parts]
    weight_ref, bias_ref, cot_ref, out_ref, grad_ref, terms_ref, wg = refs[n_parts:]
    agg_t = tree_sum([p[...] for p in parts])
    high = agg_t.astype(BF16)
    low = (agg_t - high.astype(F32)).astype(BF16)
    dims = (((0,), (0,)), ((), ()))
    weight = weight_ref[...]
    pre = lax.dot_general(high, weight, dims, preferred_element_type=F32)
    pre += lax.dot_general(low, weight, dims, preferred_element_type=F32)
    pre += bias_ref[...]
    c = math.sqrt(2.0 / math.pi)
    square = pre * pre
    t = jnp.tanh(c * pre * (1.0 + 0.044715 * square))
    half = 0.5 * (1.0 + t)
    out_ref[...] = (pre * half).astype(BF16)
    slope = half + 0.5 * pre * (1.0 - t * t) * (c * (1.0 + 3 * 0.044715 * square))
    grad = (cot_ref[...].astype(F32) * slope).astype(BF16)
    grad_ref[...] = lax.dot_general(
        grad, weight, (((1,), (1,)), ((), ())), preferred_element_type=F32
    ).astype(BF16)
    wg[...] = jnp.dot(high, grad, preferred_element_type=F32)
    wg[...] += jnp.dot(low, grad, preferred_element_type=F32)
    bias_row = jnp.sum(grad.astype(F32), axis=0, keepdims=True).astype(BF16)
    bias_rows = jnp.broadcast_to(bias_row, (PAD, bias_row.shape[1]))
    depth = wg.shape[0] // cols
    for k in range(cols):
        start = pl.multiple_of((place_ref[1] ^ k) * depth, depth)
        terms_ref[k, :depth, :] = wg[pl.ds(start, depth), :].astype(BF16)
        terms_ref[k, depth:, :] = bias_rows


def pull_kernel(rows, cols, slots, tiles, code_ref, place_ref, *refs):
    grad_refs, vals_ref, out_ref, total = refs[:rows], refs[rows], refs[rows + 1], refs[rows + 2]
    size = vals_ref.shape[-1]
    row, col = place_ref[0], place_ref[1]
    total[...] = jnp.zeros_like(total)
    for k in range(rows):
        owner = row ^ k
        for s in range(slots):
            word = code_ref[owner * slots + s]
            dest = word % 256
            live = dest < tiles
            start = pl.multiple_of(jnp.where(live, dest, 0) * size, size)
            block = grad_refs[k][pl.ds(start, size), :]
            term = jnp.dot(vals_ref[owner, s], block, preferred_element_type=F32)
            source = word // 256
            total[source] += jnp.where(live, term, 0.0)
    for k in range(cols):
        for t in range(tiles):
            out_ref[k, t * size : (t + 1) * size, :] = total[(col ^ k) * tiles + t].astype(BF16)


def last_kernel(cols, scale, place_ref, *refs):
    blocks, pieces = refs[:cols], refs[cols : 2 * cols]
    bias_ref, in_ref, wg_ref, bg_ref = refs[2 * cols :]
    in_ref[...] = tree_sum([b[...] for b in blocks]).astype(BF16)
    depth = wg_ref.shape[0] // cols
    for k in range(cols):
        start = pl.multiple_of((place_ref[1] ^ k) * depth, depth)
        wg_ref[pl.ds(start, depth), :] = pieces[k][...].astype(F32) * scale
    bg_ref[...] = bias_ref[...] * scale


def local(features, weight, bias, tile_values, tile_source, tile_dest, send_counts, cotangent):
    rows, cols = lax.axis_size("rows"), lax.axis_size("cols")
    size = tile_values.shape[-1]
    slots = tile_values.shape[3]
    nodes, width_in = features.shape
    width = weight.shape[1]
    tiles = nodes // size
    span = tiles * cols
    vals = tile_values[0, 0]
    place = jnp.stack([lax.axis_index("rows"), lax.axis_index("cols")]).astype(jnp.int32)

    live = lax.broadcasted_iota(jnp.int32, (rows, slots), 1) < send_counts[0, 0][:, None]
    code = (tile_source[0, 0] * 256 + jnp.where(live, tile_dest[0, 0], 255)).reshape(-1)

    far = [send(features, "cols", k) for k in range(cols - 1, 0, -1)][::-1]
    flops = 2 * rows * slots * size * size * width
    contrib = call(
        functools.partial(push_kernel, rows, slots, tiles, span),
        jax.ShapeDtypeStruct((rows, width_in, nodes), BF16),
        [pltpu.VMEM((span, width_in, size), BF16)],
        2,
        cols + 1,
        flops,
    )(code, place, features, *far, vals)

    pair = {k: send(contrib[k + 1], "rows", 1) for k in range(rows - 2, -1, -2)}
    parts = [contrib[0], pair[0]]
    direct = {}
    for k in range(rows - 2, 0, -2):
        both = (contrib[k].astype(F32) + pair[k].astype(F32)).astype(BF16)
        direct[k] = send(both, "rows", k)
    own = (contrib[0].astype(F32) + pair[0].astype(F32)).astype(F32)
    parts = [own] + [direct[k] for k in range(2, rows, 2)]

    depth = width_in // cols
    output, grad, terms = call(
        functools.partial(middle_kernel, cols, len(parts)),
        [
            jax.ShapeDtypeStruct((nodes, width), BF16),
            jax.ShapeDtypeStruct((nodes, width_in), BF16),
            jax.ShapeDtypeStruct((cols, depth + PAD, width), BF16),
        ],
        [pltpu.VMEM((width_in, width), F32)],
        1,
        len(parts) + 3,
        10 * width * width * nodes,
    )(place, *parts, weight, bias[None, :], cotangent)

    got = {0: grad}
    for k in range(2, rows, 2):
        got[k] = send(grad, "rows", k)
    got[1] = send(grad, "rows", 1)
    for k in range(2, rows, 2):
        got[k + 1] = send(got[k], "rows", 1)

    part = tree_sum([terms[0]] + [send(terms[k], "cols", k) for k in range(1, cols)]).astype(BF16)
    part = tree_sum([part] + [send(part, "rows", k) for k in range(2, rows, 2)]).astype(BF16)
    part = part.astype(F32) + send(part, "rows", 1).astype(F32)
    piece = part[:depth].astype(BF16)

    blocks = call(
        functools.partial(pull_kernel, rows, cols, slots, tiles),
        jax.ShapeDtypeStruct((cols, nodes, width_in), BF16),
        [pltpu.VMEM((span, size, width_in), F32)],
        2,
        rows + 1,
        flops,
    )(code, place, *[got[k] for k in range(rows)], vals)
    arrived = [blocks[0]] + [send(blocks[k], "cols", k) for k in range(1, cols)]
    pieces = [piece] + [send(piece, "cols", k) for k in range(1, cols)]
    scale = 1.0 / math.sqrt(nodes * rows * cols)
    input_grad, weight_grad, bias_grad = call(
        functools.partial(last_kernel, cols, scale),
        [
            jax.ShapeDtypeStruct((nodes, width_in), BF16),
            jax.ShapeDtypeStruct((width_in, width), F32),
            jax.ShapeDtypeStruct((1, width), F32),
        ],
        (),
        1,
        2 * cols + 1,
    )(place, *arrived, *pieces, part[depth : depth + 1])
    return output, input_grad, weight_grad, bias_grad[0]


def solution(mesh):
    in_specs = (
        P(("rows", "cols"), None),
        P(),
        P(),
        P("rows", "cols", None, None, None, None),
        P("rows", "cols", None, None),
        P("rows", "cols", None, None),
        P("rows", "cols", None),
        P(("rows", "cols"), None),
    )
    out_specs = (P(("rows", "cols"), None), P(("rows", "cols"), None), P(), P())
    return jax.shard_map(local, mesh=mesh, in_specs=in_specs, out_specs=out_specs, check_vma=False)
```

```python
import functools
import math

import jax
import jax.numpy as jnp
from jax import lax
from jax.experimental import pallas as pl
from jax.experimental.pallas import tpu as pltpu
from jax.sharding import PartitionSpec as P

F32 = jnp.float32
BF16 = jnp.bfloat16
PAD = 16


def call(body, out_shape, scratch=(), n_smem=0, n_vmem=0, flops=0, n_any=0):
    specs = [pl.BlockSpec(memory_space=pltpu.SMEM)] * n_smem
    specs += [pl.BlockSpec(memory_space=pltpu.VMEM)] * n_vmem
    specs += [pl.BlockSpec(memory_space=pl.ANY)] * n_any
    many = isinstance(out_shape, (list, tuple))
    vmem = pl.BlockSpec(memory_space=pltpu.VMEM)
    return pl.pallas_call(
        body,
        out_shape=out_shape,
        in_specs=specs,
        out_specs=[vmem] * len(out_shape) if many else vmem,
        scratch_shapes=list(scratch),
        cost_estimate=pl.CostEstimate(flops=flops, bytes_accessed=2_000_000, transcendentals=0),
        compiler_params=pltpu.CompilerParams(vmem_limit_bytes=48 * 1024 * 1024),
    )


def tree_sum(items):
    items = [x.astype(F32) for x in items]
    while len(items) > 1:
        items = [sum(items[i + 1 : i + 2], items[i]) for i in range(0, len(items), 2)]
    return items[0]


def send(x, axis, offset):
    size = lax.axis_size(axis)
    return lax.ppermute(x, axis, [(i, i ^ offset) for i in range(size)])


def prepare_kernel(
    tiles, source_hbm, dest_hbm, count_hbm, feat_hbm, vals_hbm, picked_ref, own_ref, code_ref,
    source_ref, dest_ref, count_ref, feat, vals, sems,
):
    rows, slots, size, _ = vals.shape
    small = [(source_hbm, source_ref), (dest_hbm, dest_ref), (count_hbm, count_ref), (feat_hbm, feat)]
    copies = [pltpu.make_async_copy(x, y, sems.at[i]) for i, (x, y) in enumerate(small)]
    copies += [
        pltpu.make_async_copy(vals_hbm.at[o], vals.at[o], sems.at[len(small) + o]) for o in range(rows)
    ]
    for copy in copies:
        copy.start()
    for copy in copies[: len(small)]:
        copy.wait()
    for o in range(rows):
        for s in range(slots):
            code_ref[o * slots + s] = source_ref[0, s, 0, o]
    for k in range(tiles):
        own_ref[k] = feat[k * size : (k + 1) * size, :].T
    for o in range(rows):
        copies[len(small) + o].wait()
        for s in range(slots):
            live = s < count_ref[0, 0, o]
            dest = jnp.where(live, dest_ref[0, s, 0, o], tiles)
            block = vals[o, s]
            zero = jnp.zeros_like(block)
            for t in range(tiles):
                picked_ref[o, s, :, t * size : (t + 1) * size] = jnp.where(dest == t, block, zero)


def push_one(k, place_ref, code_ref, turned, picked_ref):
    owner = place_ref[0] ^ k
    total = None
    for s in range(picked_ref.shape[1]):
        part = jnp.dot(
            turned[code_ref[owner * picked_ref.shape[1] + s]], picked_ref[owner, s], preferred_element_type=F32
        )
        total = part if total is None else total + part
    return total.astype(BF16)


def push_first_kernel(ks, tiles, place_ref, code_ref, *refs):
    n = len(refs) - len(ks) - 1
    own_ref, far, picked_ref = refs[0], refs[1 : n - 1], refs[n - 1]
    outs, turned = refs[n:-1], refs[-1]
    size = picked_ref.shape[2]
    col = place_ref[1]
    for t in range(tiles):
        turned[col * tiles + t] = own_ref[t]
    for k, ref in enumerate(far, 1):
        for t in range(tiles):
            turned[(col ^ k) * tiles + t] = ref[t * size : (t + 1) * size, :].T
    for k, out_ref in zip(ks, outs):
        out_ref[...] = push_one(k, place_ref, code_ref, turned, picked_ref)


def push_second_kernel(ks, place_ref, code_ref, turned, picked_ref, *outs):
    for k, out_ref in zip(ks, outs):
        out_ref[...] = push_one(k, place_ref, code_ref, turned, picked_ref)


def add_kernel(*refs):
    refs[-1][...] = tree_sum([r[...] for r in refs[:-1]]).astype(refs[-1].dtype)


def middle_kernel(n_parts, place_ref, *refs):
    parts = refs[:n_parts]
    weight_ref, bias_ref, cot_ref, back_ref, pre_ref = refs[n_parts : n_parts + 5]
    terms, wg = refs[n_parts + 5 : -1], refs[-1]
    agg = tree_sum([p[...] for p in parts])
    high = agg.astype(BF16)
    low = (agg - high.astype(F32)).astype(BF16)
    dims = (((0,), (0,)), ((), ()))
    weight = weight_ref[...]
    pre = lax.dot_general(high, weight, dims, preferred_element_type=F32)
    pre += lax.dot_general(low, weight, dims, preferred_element_type=F32)
    pre += bias_ref[...]
    pre_ref[...] = pre
    c = math.sqrt(2.0 / math.pi)
    square = pre * pre
    t = jnp.tanh(c * pre * (1.0 + 0.044715 * square))
    slope = 0.5 * (1.0 + t) + 0.5 * pre * (1.0 - t * t) * (c * (1.0 + 3 * 0.044715 * square))
    grad = (cot_ref[...].astype(F32) * slope).astype(BF16)
    back_ref[...] = lax.dot_general(
        grad, weight, (((1,), (1,)), ((), ())), preferred_element_type=F32
    ).astype(BF16)
    wg[...] = jnp.dot(high, grad, preferred_element_type=F32)
    bias_row = jnp.sum(grad.astype(F32), axis=0, keepdims=True).astype(BF16)
    bias_rows = jnp.broadcast_to(bias_row, (PAD, bias_row.shape[1]))
    depth = wg.shape[0] // len(terms)
    for k, part in enumerate(terms):
        start = pl.multiple_of((place_ref[1] ^ k) * depth, depth)
        part[:depth, :] = wg[pl.ds(start, depth), :].astype(BF16)
        part[depth:, :] = bias_rows


def output_kernel(pre_ref, out_ref):
    pre = pre_ref[...]
    c = math.sqrt(2.0 / math.pi)
    t = jnp.tanh(c * pre * (1.0 + 0.044715 * pre * pre))
    out_ref[...] = (pre * (0.5 * (1.0 + t))).astype(BF16)


def pack_kernel(n_after, block_ref, *refs):
    part_ref, packed_ref = refs[-2:]
    part = tree_sum([r[...] for r in refs[: -2 - n_after]]).astype(BF16)
    part_ref[...] = part
    nodes = block_ref.shape[0]
    packed_ref[:nodes, :] = block_ref[...]
    packed_ref[nodes:, :] = part


def unpack_kernel(part_ref, packed_ref, out_ref):
    below = packed_ref.shape[0] - part_ref.shape[0]
    out_ref[...] = (part_ref[...].astype(F32) + packed_ref[below:, :].astype(F32)).astype(BF16)


def pull_kernel(rows, cols, tiles, place_ref, code_ref, *refs):
    grad_refs, picked_ref, outs, total = refs[:rows], refs[rows], refs[rows + 2 : -1], refs[-1]
    slots, size = picked_ref.shape[1], picked_ref.shape[2]
    row, col = place_ref[0], place_ref[1]
    total[...] = jnp.zeros_like(total)
    for k in range(rows):
        owner = row ^ k
        block = grad_refs[k][: tiles * size, :]
        for s in range(slots):
            total[code_ref[owner * picked_ref.shape[1] + s]] += jnp.dot(
                picked_ref[owner, s], block, preferred_element_type=F32
            )
    for k in range(cols):
        for t in range(tiles):
            outs[k][t * size : (t + 1) * size, :] = total[(col ^ k) * tiles + t].astype(BF16)


def last_kernel(cols, n_blocks, scale, place_ref, *refs):
    blocks, pieces = refs[:n_blocks], refs[n_blocks : n_blocks + cols]
    bias_ref, in_ref, wg_ref, bg_ref = refs[n_blocks + cols :]
    total = blocks[0][...].astype(F32)
    for b in blocks[1:]:
        total += b[...].astype(F32)
    in_ref[...] = total.astype(BF16)
    depth = wg_ref.shape[0] // cols
    for k in range(cols):
        start = pl.multiple_of((place_ref[1] ^ k) * depth, depth)
        wg_ref[pl.ds(start, depth), :] = pieces[k][...].astype(F32) * scale
    bg_ref[...] = bias_ref[...].astype(F32) * scale


def local(features, weight, bias, tile_values, tile_source, tile_dest, send_counts, cotangent):
    rows, cols = lax.axis_size("rows"), lax.axis_size("cols")
    size = tile_values.shape[-1]
    slots = tile_values.shape[3]
    nodes, width_in = features.shape
    width = weight.shape[1]
    tiles = nodes // size
    span = tiles * cols
    vals = tile_values[0, 0]
    place = jnp.stack([lax.axis_index("rows"), lax.axis_index("cols")]).astype(jnp.int32)
    source = tile_source.transpose(0, 3, 1, 2)
    dest = tile_dest.transpose(0, 3, 1, 2)
    shape = jax.ShapeDtypeStruct
    block = shape((width_in, nodes), BF16)
    flops = rows * slots * size * size * tiles * width

    far = {k: send(features, "cols", k) for k in range(cols - 1, 0, -1)}
    hbm, smem = pl.BlockSpec(memory_space=pltpu.HBM), pl.BlockSpec(memory_space=pltpu.SMEM)
    vmem = pl.BlockSpec(memory_space=pltpu.VMEM)
    picked, own, code = pl.pallas_call(
        functools.partial(prepare_kernel, tiles),
        out_shape=[
            shape((rows, slots, size, tiles * size), BF16),
            shape((tiles, width_in, size), BF16),
            shape((rows * slots,), jnp.int32),
        ],
        in_specs=[hbm] * 5,
        out_specs=[vmem, vmem, smem],
        scratch_shapes=[
            pltpu.SMEM(source.shape, jnp.int32),
            pltpu.SMEM(dest.shape, jnp.int32),
            pltpu.SMEM(send_counts.shape, jnp.int32),
            pltpu.VMEM(features.shape, BF16),
            pltpu.VMEM(vals.shape, BF16),
            pltpu.SemaphoreType.DMA((4 + rows,)),
        ],
        cost_estimate=pl.CostEstimate(flops=flops, bytes_accessed=2_000_000, transcendentals=0),
        compiler_params=pltpu.CompilerParams(vmem_limit_bytes=48 * 1024 * 1024),
    )(source, dest, send_counts, features, vals)

    odd = list(range(rows - 1, 0, -2))
    even = list(range(rows - 2, -1, -2))
    *sent, turned = call(
        functools.partial(push_first_kernel, odd, tiles),
        [block] * len(odd) + [shape((span, width_in, size), BF16)],
        n_smem=2,
        n_vmem=cols + 1,
        flops=flops,
    )(place, code, own, *[far[k] for k in range(1, cols)], picked)
    kept = call(
        functools.partial(push_second_kernel, even),
        [block] * len(even),
        n_smem=2,
        n_vmem=2,
        flops=flops,
    )(place, code, turned, picked)

    summed = {k: [kept_k, send(sent_k, "rows", 1)] for k, kept_k, sent_k in zip(even, kept, sent)}
    bit = 2
    while bit < rows:
        for k in range(rows - bit, 0, -2 * bit):
            n = len(summed[k])
            both = call(add_kernel, block, n_vmem=n)(*summed.pop(k))
            summed[k ^ bit].append(send(both, "rows", bit))
        bit *= 2
    parts = summed[0]

    depth = width_in // cols
    part_shape = shape((depth + PAD, width), BF16)
    back, pre, *terms = call(
        functools.partial(middle_kernel, len(parts)),
        [shape((nodes, width_in), BF16), shape((nodes, width), F32)] + [part_shape] * cols,
        [pltpu.VMEM((width_in, width), F32)],
        1,
        len(parts) + 3,
        8 * width * width * nodes,
    )(place, *parts, weight, bias[None, :], cotangent)

    got = {0: back}
    bit = rows // 2
    while bit > 1:
        for k in sorted(got):
            got[k ^ bit] = send(got[k], "rows", bit)
        bit //= 2
    for k in range(0, rows - 2, 2):
        got[k + 1] = send(got[k], "rows", 1)

    output = call(output_kernel, shape((nodes, width), BF16), n_vmem=1)(pre)

    after = [got[k] for k in range(1, rows - 2, 2)]
    part, packed = call(
        functools.partial(pack_kernel, len(after)),
        [part_shape, shape((nodes + depth + PAD, width), BF16)],
        n_vmem=cols + 1,
        n_any=len(after),
    )(got[rows - 2], terms[0], *[send(terms[k], "cols", k) for k in range(cols - 1, 0, -1)][::-1], *after)
    got[rows - 1] = send(packed, "rows", 1)
    part = call(unpack_kernel, part_shape, n_vmem=2)(part, got[rows - 1])
    others = [send(part, "rows", k) for k in range(2, rows, 2)]

    blocks = call(
        functools.partial(pull_kernel, rows, cols, tiles),
        [shape((nodes, width_in), BF16)] * cols,
        [pltpu.VMEM((span, size, width_in), F32)],
        2,
        rows + 1,
        flops,
        n_any=1,
    )(place, code, *[got[k] for k in range(rows)], picked, part)
    arrived = [blocks[0]]
    for k in range(cols - 2, 0, -2):
        near = send(blocks[k + 1], "cols", 1)
        both = call(add_kernel, shape((nodes, width_in), BF16), n_vmem=2)(blocks[k], near)
        arrived.append(send(both, "cols", k))
    arrived.append(send(blocks[1], "cols", 1))
    part = call(add_kernel, part_shape, n_vmem=rows // 2)(part, *others)
    piece = part[:depth]
    pieces = [piece] + [send(piece, "cols", k) for k in range(cols - 1, 0, -1)][::-1]
    scale = 1.0 / math.sqrt(nodes * rows * cols)
    input_grad, weight_grad, bias_grad = call(
        functools.partial(last_kernel, cols, len(arrived), scale),
        [
            shape((nodes, width_in), BF16),
            shape((width_in, width), F32),
            shape((1, width), F32),
        ],
        n_smem=1,
        n_vmem=len(arrived) + cols + 1,
    )(place, *arrived, *pieces, part[depth : depth + 1])
    return output, input_grad, weight_grad, bias_grad[0]


def solution(mesh):
    in_specs = (
        P(("rows", "cols"), None),
        P(),
        P(),
        P("rows", "cols", None, None, None, None),
        P("rows", "cols", None, None),
        P("rows", "cols", None, None),
        P("rows", "cols", None),
        P(("rows", "cols"), None),
    )
    out_specs = (P(("rows", "cols"), None), P(("rows", "cols"), None), P(), P())
    return jax.shard_map(local, mesh=mesh, in_specs=in_specs, out_specs=out_specs, check_vma=False)
```

```python
import functools
import math

import jax
import jax.numpy as jnp
from jax import lax
from jax.experimental import pallas as pl
from jax.experimental.pallas import tpu as pltpu
from jax.sharding import PartitionSpec as P

F32 = jnp.float32
BF16 = jnp.bfloat16
PAD = 16


def call(body, out_shape, scratch=(), n_smem=0, n_vmem=0, flops=0, n_any=0):
    specs = [pl.BlockSpec(memory_space=pltpu.SMEM)] * n_smem
    specs += [pl.BlockSpec(memory_space=pltpu.VMEM)] * n_vmem
    specs += [pl.BlockSpec(memory_space=pl.ANY)] * n_any
    many = isinstance(out_shape, (list, tuple))
    vmem = pl.BlockSpec(memory_space=pltpu.VMEM)
    return pl.pallas_call(
        body,
        out_shape=out_shape,
        in_specs=specs,
        out_specs=[vmem] * len(out_shape) if many else vmem,
        scratch_shapes=list(scratch),
        cost_estimate=pl.CostEstimate(flops=flops, bytes_accessed=2_000_000, transcendentals=0),
        compiler_params=pltpu.CompilerParams(vmem_limit_bytes=48 * 1024 * 1024),
    )


def tree_sum(items):
    items = [x.astype(F32) for x in items]
    while len(items) > 1:
        items = [sum(items[i + 1 : i + 2], items[i]) for i in range(0, len(items), 2)]
    return items[0]


def send(x, axis, offset):
    size = lax.axis_size(axis)
    return lax.ppermute(x, axis, [(i, i ^ offset) for i in range(size)])


def prepare_kernel(
    tiles, source_ref, dest_ref, count_ref, feat_ref, vals_ref, picked_ref, own_ref, code_ref
):
    rows, slots, size, _ = vals_ref.shape
    for o in range(rows):
        for s in range(slots):
            code_ref[o * slots + s] = source_ref[0, s, 0, o]
    for k in range(tiles):
        own_ref[k] = feat_ref[k * size : (k + 1) * size, :].T
    for o in range(rows):
        for s in range(slots):
            live = s < count_ref[0, 0, o]
            dest = jnp.where(live, dest_ref[0, s, 0, o], tiles)
            block = vals_ref[o, s]
            zero = jnp.zeros_like(block)
            for t in range(tiles):
                picked_ref[o, s, :, t * size : (t + 1) * size] = jnp.where(dest == t, block, zero)


def push_one(k, place_ref, code_ref, turned, picked_ref):
    owner = place_ref[0] ^ k
    _, slots, size, wide = picked_ref.shape
    sources = jnp.concatenate([turned[code_ref[owner * slots + s]] for s in range(slots)], axis=1)
    chosen = picked_ref[owner].reshape(slots * size, wide)
    return jnp.dot(sources, chosen, preferred_element_type=F32).astype(BF16)


def push_first_kernel(ks, tiles, place_ref, code_ref, *refs):
    n = len(refs) - len(ks) - 1
    own_ref, far, picked_ref = refs[0], refs[1 : n - 1], refs[n - 1]
    outs, turned = refs[n:-1], refs[-1]
    size = picked_ref.shape[2]
    col = place_ref[1]
    for t in range(tiles):
        turned[col * tiles + t] = own_ref[t]
    for k, ref in enumerate(far, 1):
        for t in range(tiles):
            turned[(col ^ k) * tiles + t] = ref[t * size : (t + 1) * size, :].T
    for k, out_ref in zip(ks, outs):
        out_ref[...] = push_one(k, place_ref, code_ref, turned, picked_ref)


def push_second_kernel(ks, place_ref, code_ref, turned, picked_ref, *outs):
    for k, out_ref in zip(ks, outs):
        out_ref[...] = push_one(k, place_ref, code_ref, turned, picked_ref)


def add_kernel(*refs):
    refs[-1][...] = tree_sum([r[...] for r in refs[:-1]]).astype(refs[-1].dtype)


def middle_kernel(n_parts, place_ref, *refs):
    parts = refs[:n_parts]
    weight_ref, bias_ref, cot_ref, back_ref, pre_ref, keep_ref, away_ref, wg = refs[n_parts:]
    agg = tree_sum([p[...] for p in parts])
    high = agg.astype(BF16)
    low = (agg - high.astype(F32)).astype(BF16)
    dims = (((0,), (0,)), ((), ()))
    weight = weight_ref[...]
    pre = lax.dot_general(high, weight, dims, preferred_element_type=F32)
    pre += lax.dot_general(low, weight, dims, preferred_element_type=F32)
    pre += bias_ref[...]
    pre_ref[...] = pre
    c = math.sqrt(2.0 / math.pi)
    square = pre * pre
    t = jnp.tanh(c * pre * (1.0 + 0.044715 * square))
    slope = 0.5 * (1.0 + t) + 0.5 * pre * (1.0 - t * t) * (c * (1.0 + 3 * 0.044715 * square))
    grad = (cot_ref[...].astype(F32) * slope).astype(BF16)
    back_ref[...] = lax.dot_general(
        grad, weight, (((1,), (1,)), ((), ())), preferred_element_type=F32
    ).astype(BF16)
    wg[...] = jnp.dot(high, grad, preferred_element_type=F32)
    bias_row = jnp.sum(grad.astype(F32), axis=0, keepdims=True).astype(BF16)
    bias_rows = jnp.broadcast_to(bias_row, (PAD, bias_row.shape[1]))
    depth = wg.shape[0] // 2
    mine = place_ref[1] % 2
    for which, ref in ((mine, keep_ref), (1 - mine, away_ref)):
        ref[:depth, :] = wg[pl.ds(pl.multiple_of(which * depth, depth), depth), :].astype(BF16)
        ref[depth:, :] = bias_rows


def output_kernel(pre_ref, out_ref):
    pre = pre_ref[...]
    c = math.sqrt(2.0 / math.pi)
    t = jnp.tanh(c * pre * (1.0 + 0.044715 * pre * pre))
    out_ref[...] = (pre * (0.5 * (1.0 + t))).astype(BF16)


def pack_kernel(block_ref, part_ref, *refs):
    out_ref = refs[-1]
    nodes = part_ref.shape[0]
    out_ref[:-nodes, :] = block_ref[...]
    out_ref[-nodes:, :] = part_ref[...]


def repack_kernel(packed_ref, part_ref, *refs):
    sum_ref, out_ref = refs[-2:]
    depth = part_ref.shape[0]
    nodes = packed_ref.shape[0] - depth
    total = (part_ref[...].astype(F32) + packed_ref[nodes:, :].astype(F32)).astype(BF16)
    sum_ref[...] = total
    out_ref[:nodes, :] = packed_ref[:nodes, :]
    out_ref[nodes:, :] = total


def unpack_kernel(packed_ref, part_ref, sum_ref):
    nodes = packed_ref.shape[0] - part_ref.shape[0]
    sum_ref[...] = (part_ref[...].astype(F32) + packed_ref[nodes:, :].astype(F32)).astype(BF16)


def pull_kernel(rows, cols, tiles, place_ref, code_ref, *refs):
    grad_refs, picked_ref, outs, total = refs[:rows], refs[rows], refs[rows + 2 : -1], refs[-1]
    slots, size = picked_ref.shape[1], picked_ref.shape[2]
    row, col = place_ref[0], place_ref[1]
    total[...] = jnp.zeros_like(total)
    for k in range(rows):
        owner = row ^ k
        block = grad_refs[k][: tiles * size, :]
        terms = jnp.dot(
            picked_ref[owner].reshape(slots * size, block.shape[0]), block, preferred_element_type=F32
        )
        for s in range(slots):
            total[code_ref[owner * slots + s]] += terms[s * size : (s + 1) * size]
    for k in range(cols):
        for t in range(tiles):
            outs[k][t * size : (t + 1) * size, :] = total[(col ^ k) * tiles + t].astype(BF16)


def last_kernel(n_blocks, scale, place_ref, *refs):
    blocks = refs[:n_blocks]
    part_ref, other_ref, in_ref, wg_ref, bg_ref = refs[n_blocks:]
    in_ref[...] = tree_sum([b[...] for b in blocks]).astype(BF16)
    depth = other_ref.shape[0]
    mine = place_ref[1] % 2
    for which, ref in ((mine, part_ref), (1 - mine, other_ref)):
        start = pl.multiple_of(which * depth, depth)
        wg_ref[pl.ds(start, depth), :] = ref[:depth, :].astype(F32) * scale
    bg_ref[...] = part_ref[depth : depth + 1, :].astype(F32) * scale


def local(features, weight, bias, tile_values, tile_source, tile_dest, send_counts, cotangent):
    rows, cols = lax.axis_size("rows"), lax.axis_size("cols")
    size = tile_values.shape[-1]
    slots = tile_values.shape[3]
    nodes, width_in = features.shape
    width = weight.shape[1]
    tiles = nodes // size
    span = tiles * cols
    vals = tile_values[0, 0]
    place = jnp.stack([lax.axis_index("rows"), lax.axis_index("cols")]).astype(jnp.int32)
    source = tile_source.transpose(0, 3, 1, 2)
    dest = tile_dest.transpose(0, 3, 1, 2)
    shape = jax.ShapeDtypeStruct
    block = shape((width_in, nodes), BF16)
    flops = rows * slots * size * size * tiles * width

    far = {k: send(features, "cols", k) for k in range(cols - 1, 0, -1)}
    smem, vmem = pl.BlockSpec(memory_space=pltpu.SMEM), pl.BlockSpec(memory_space=pltpu.VMEM)
    picked, own, code = pl.pallas_call(
        functools.partial(prepare_kernel, tiles),
        out_shape=[
            shape((rows, slots, size, tiles * size), BF16),
            shape((tiles, width_in, size), BF16),
            shape((rows * slots,), jnp.int32),
        ],
        in_specs=[smem] * 3 + [vmem] * 2,
        out_specs=[vmem, vmem, smem],
        cost_estimate=pl.CostEstimate(flops=flops, bytes_accessed=2_000_000, transcendentals=0),
        compiler_params=pltpu.CompilerParams(vmem_limit_bytes=48 * 1024 * 1024),
    )(source, dest, send_counts, features, vals)

    odd = list(range(rows - 1, 0, -2))
    even = list(range(rows - 2, -1, -2))
    *sent, turned = call(
        functools.partial(push_first_kernel, odd, tiles),
        [block] * len(odd) + [shape((span, width_in, size), BF16)],
        n_smem=2,
        n_vmem=cols + 1,
        flops=flops,
    )(place, code, own, *[far[k] for k in range(1, cols)], picked)
    kept = call(
        functools.partial(push_second_kernel, even),
        [block] * len(even),
        n_smem=2,
        n_vmem=2,
        flops=flops,
    )(place, code, turned, picked)

    summed = {k: [kept_k, send(sent_k, "rows", 1)] for k, kept_k, sent_k in zip(even, kept, sent)}
    bit = 2
    while bit < rows:
        for k in range(rows - bit, 0, -2 * bit):
            n = len(summed[k])
            both = call(add_kernel, block, n_vmem=n)(*summed.pop(k))
            summed[k ^ bit].append(send(both, "rows", bit))
        bit *= 2
    parts = summed[0]

    depth = width_in // 2
    part_shape = shape((depth + PAD, width), BF16)
    back, pre, part, away = call(
        functools.partial(middle_kernel, len(parts)),
        [shape((nodes, width_in), BF16), shape((nodes, width), F32), part_shape, part_shape],
        [pltpu.VMEM((width_in, width), F32)],
        1,
        len(parts) + 3,
        8 * width * width * nodes,
    )(place, *parts, weight, bias[None, :], cotangent)
    output = call(output_kernel, shape((nodes, width), BF16), n_vmem=1)(pre)

    part = call(add_kernel, part_shape, n_vmem=2)(part, send(away, "cols", 1))
    bit = 2
    while bit < cols:
        part = call(add_kernel, part_shape, n_vmem=2)(part, send(part, "cols", bit))
        bit *= 2

    got = {0: back, 1: send(back, "rows", 1)}
    packed_shape = shape((nodes + depth + PAD, width), BF16)
    bit = rows // 2
    while bit > 1:
        for k in sorted(k for k in got if k % 2 == 0):
            if k ^ bit == rows - 2:
                packed = call(pack_kernel, packed_shape, n_vmem=2, n_any=1)(got[k], part, got[1])
                got[k ^ bit] = send(packed, "rows", bit)
            else:
                got[k ^ bit] = send(got[k], "rows", bit)
        bit //= 2
    for k in range(2, rows - 2, 2):
        got[k + 1] = send(got[k], "rows", 1)
    others = [got[k] for k in range(1, rows - 2, 2)]
    part, packed = call(
        repack_kernel, [part_shape, packed_shape], n_vmem=2, n_any=len(others)
    )(got[rows - 2], part, *others)
    got[rows - 1] = send(packed, "rows", 1)
    part = call(unpack_kernel, part_shape, n_vmem=2)(got[rows - 1], part)
    after = part
    bit = 4
    while bit < rows:
        part = call(add_kernel, part_shape, n_vmem=2)(part, send(part, "rows", bit))
        bit *= 2
    half = part[:depth]
    other = send(half, "cols", 1)

    blocks = call(
        functools.partial(pull_kernel, rows, cols, tiles),
        [shape((nodes, width_in), BF16)] * cols,
        [pltpu.VMEM((span, size, width_in), F32)],
        2,
        rows + 1,
        flops,
        n_any=1,
    )(place, code, *[got[k] for k in range(rows)], picked, after)
    arrived = [blocks[0]]
    for k in range(cols - 2, 0, -2):
        near = send(blocks[k + 1], "cols", 1)
        both = call(add_kernel, shape((nodes, width_in), BF16), n_vmem=2)(blocks[k], near)
        arrived.append(send(both, "cols", k))
    arrived.append(send(blocks[1], "cols", 1))
    scale = 1.0 / math.sqrt(nodes * rows * cols)
    input_grad, weight_grad, bias_grad = call(
        functools.partial(last_kernel, len(arrived), scale),
        [
            shape((nodes, width_in), BF16),
            shape((width_in, width), F32),
            shape((1, width), F32),
        ],
        n_smem=1,
        n_vmem=len(arrived) + 2,
    )(place, *arrived, part, other)
    return output, input_grad, weight_grad, bias_grad[0]


def solution(mesh):
    in_specs = (
        P(("rows", "cols"), None),
        P(),
        P(),
        P("rows", "cols", None, None, None, None),
        P("rows", "cols", None, None),
        P("rows", "cols", None, None),
        P("rows", "cols", None),
        P(("rows", "cols"), None),
    )
    out_specs = (P(("rows", "cols"), None), P(("rows", "cols"), None), P(), P())
    return jax.shard_map(local, mesh=mesh, in_specs=in_specs, out_specs=out_specs, check_vma=False)
```

```python
import functools
import math

import jax
import jax.numpy as jnp
from jax import lax
from jax.experimental import pallas as pl
from jax.experimental.pallas import tpu as pltpu
from jax.sharding import PartitionSpec as P

F32 = jnp.float32
BF16 = jnp.bfloat16
PAD = 16


def call(body, out_shape, scratch=(), n_smem=0, n_vmem=0, flops=0, n_any=0):
    specs = [pl.BlockSpec(memory_space=pltpu.SMEM)] * n_smem
    specs += [pl.BlockSpec(memory_space=pltpu.VMEM)] * n_vmem
    specs += [pl.BlockSpec(memory_space=pl.ANY)] * n_any
    many = isinstance(out_shape, (list, tuple))
    vmem = pl.BlockSpec(memory_space=pltpu.VMEM)
    return pl.pallas_call(
        body,
        out_shape=out_shape,
        in_specs=specs,
        out_specs=[vmem] * len(out_shape) if many else vmem,
        scratch_shapes=list(scratch),
        cost_estimate=pl.CostEstimate(flops=flops, bytes_accessed=2_000_000, transcendentals=0),
        compiler_params=pltpu.CompilerParams(vmem_limit_bytes=48 * 1024 * 1024),
    )


def tree_sum(items):
    items = [x.astype(F32) for x in items]
    while len(items) > 1:
        items = [sum(items[i + 1 : i + 2], items[i]) for i in range(0, len(items), 2)]
    return items[0]


def send(x, axis, offset):
    size = lax.axis_size(axis)
    return lax.ppermute(x, axis, [(i, i ^ offset) for i in range(size)])


def prepare_kernel(
    tiles, source_ref, dest_ref, count_ref, feat_ref, vals_ref, picked_ref, own_ref, code_ref
):
    rows, slots, size, _ = vals_ref.shape
    for o in range(rows):
        for s in range(slots):
            code_ref[o * slots + s] = source_ref[0, s, 0, o]
    for k in range(tiles):
        own_ref[k] = feat_ref[k * size : (k + 1) * size, :].T
    for o in range(rows):
        for s in range(slots):
            live = s < count_ref[0, 0, o]
            dest = jnp.where(live, dest_ref[0, s, 0, o], tiles)
            block = vals_ref[o, s]
            zero = jnp.zeros_like(block)
            for t in range(tiles):
                picked_ref[o, s, :, t * size : (t + 1) * size] = jnp.where(dest == t, block, zero)


def push_one(k, place_ref, code_ref, turned, picked_ref):
    owner = place_ref[0] ^ k
    _, slots, size, wide = picked_ref.shape
    sources = jnp.concatenate([turned[code_ref[owner * slots + s]] for s in range(slots)], axis=1)
    chosen = picked_ref[owner].reshape(slots * size, wide)
    return jnp.dot(sources, chosen, preferred_element_type=F32).astype(BF16)


def push_first_kernel(ks, tiles, place_ref, code_ref, *refs):
    n = len(refs) - len(ks) - 1
    own_ref, far, picked_ref = refs[0], refs[1 : n - 1], refs[n - 1]
    outs, turned = refs[n:-1], refs[-1]
    size = picked_ref.shape[2]
    col = place_ref[1]
    for t in range(tiles):
        turned[col * tiles + t] = own_ref[t]
    for k, ref in enumerate(far, 1):
        for t in range(tiles):
            turned[(col ^ k) * tiles + t] = ref[t * size : (t + 1) * size, :].T
    for k, out_ref in zip(ks, outs):
        out_ref[...] = push_one(k, place_ref, code_ref, turned, picked_ref)


def push_second_kernel(ks, place_ref, code_ref, turned, picked_ref, *outs):
    for k, out_ref in zip(ks, outs):
        out_ref[...] = push_one(k, place_ref, code_ref, turned, picked_ref)


def add_kernel(*refs):
    refs[-1][...] = tree_sum([r[...] for r in refs[:-1]]).astype(refs[-1].dtype)


def middle_kernel(n_parts, place_ref, *refs):
    parts = refs[:n_parts]
    weight_ref, bias_ref, cot_ref, back_ref, pre_ref, keep_ref, away_ref, wg = refs[n_parts:]
    agg = tree_sum([p[...] for p in parts])
    high = agg.astype(BF16)
    low = (agg - high.astype(F32)).astype(BF16)
    dims = (((0,), (0,)), ((), ()))
    weight = weight_ref[...]
    pre = lax.dot_general(high, weight, dims, preferred_element_type=F32)
    pre += lax.dot_general(low, weight, dims, preferred_element_type=F32)
    pre += bias_ref[...]
    pre_ref[...] = pre
    c = math.sqrt(2.0 / math.pi)
    square = pre * pre
    t = jnp.tanh(c * pre * (1.0 + 0.044715 * square))
    slope = 0.5 * (1.0 + t) + 0.5 * pre * (1.0 - t * t) * (c * (1.0 + 3 * 0.044715 * square))
    grad = (cot_ref[...].astype(F32) * slope).astype(BF16)
    back_ref[...] = lax.dot_general(
        grad, weight, (((1,), (1,)), ((), ())), preferred_element_type=F32
    ).astype(BF16)
    wg[...] = jnp.dot(high, grad, preferred_element_type=F32)
    bias_row = jnp.sum(grad.astype(F32), axis=0, keepdims=True).astype(BF16)
    bias_rows = jnp.broadcast_to(bias_row, (PAD, bias_row.shape[1]))
    depth = wg.shape[0] // 2
    mine = place_ref[1] % 2
    for which, ref in ((mine, keep_ref), (1 - mine, away_ref)):
        ref[:depth, :] = wg[pl.ds(pl.multiple_of(which * depth, depth), depth), :].astype(BF16)
        ref[depth:, :] = bias_rows


def output_kernel(pre_ref, out_ref):
    pre = pre_ref[...]
    c = math.sqrt(2.0 / math.pi)
    t = jnp.tanh(c * pre * (1.0 + 0.044715 * pre * pre))
    out_ref[...] = (pre * (0.5 * (1.0 + t))).astype(BF16)


def after_add_kernel(a_ref, b_ref, *refs):
    refs[-1][...] = (a_ref[...].astype(F32) + b_ref[...].astype(F32)).astype(BF16)


def pull_kernel(rows, cols, tiles, place_ref, code_ref, *refs):
    grad_refs, picked_ref, outs, total = refs[:rows], refs[rows], refs[rows + 2 : -1], refs[-1]
    slots, size = picked_ref.shape[1], picked_ref.shape[2]
    row, col = place_ref[0], place_ref[1]
    total[...] = jnp.zeros_like(total)
    for k in range(rows):
        owner = row ^ k
        block = grad_refs[k][: tiles * size, :]
        terms = jnp.dot(
            picked_ref[owner].reshape(slots * size, block.shape[0]), block, preferred_element_type=F32
        )
        for s in range(slots):
            total[code_ref[owner * slots + s]] += terms[s * size : (s + 1) * size]
    for k in range(cols):
        for t in range(tiles):
            outs[k][t * size : (t + 1) * size, :] = total[(col ^ k) * tiles + t].astype(BF16)


def last_kernel(n_blocks, scale, place_ref, *refs):
    blocks = refs[:n_blocks]
    part_ref, other_ref, in_ref, wg_ref, bg_ref = refs[n_blocks:]
    in_ref[...] = tree_sum([b[...] for b in blocks]).astype(BF16)
    depth = other_ref.shape[0]
    mine = place_ref[1] % 2
    for which, ref in ((mine, part_ref), (1 - mine, other_ref)):
        start = pl.multiple_of(which * depth, depth)
        wg_ref[pl.ds(start, depth), :] = ref[:depth, :].astype(F32) * scale
    bg_ref[...] = part_ref[depth : depth + 1, :].astype(F32) * scale


def local(features, weight, bias, tile_values, tile_source, tile_dest, send_counts, cotangent):
    rows, cols = lax.axis_size("rows"), lax.axis_size("cols")
    size = tile_values.shape[-1]
    slots = tile_values.shape[3]
    nodes, width_in = features.shape
    width = weight.shape[1]
    tiles = nodes // size
    span = tiles * cols
    vals = tile_values[0, 0]
    place = jnp.stack([lax.axis_index("rows"), lax.axis_index("cols")]).astype(jnp.int32)
    source = tile_source.transpose(0, 3, 1, 2)
    dest = tile_dest.transpose(0, 3, 1, 2)
    shape = jax.ShapeDtypeStruct
    block = shape((width_in, nodes), BF16)
    flops = rows * slots * size * size * tiles * width

    far = {k: send(features, "cols", k) for k in range(cols - 1, 0, -1)}
    smem, vmem = pl.BlockSpec(memory_space=pltpu.SMEM), pl.BlockSpec(memory_space=pltpu.VMEM)
    picked, own, code = pl.pallas_call(
        functools.partial(prepare_kernel, tiles),
        out_shape=[
            shape((rows, slots, size, tiles * size), BF16),
            shape((tiles, width_in, size), BF16),
            shape((rows * slots,), jnp.int32),
        ],
        in_specs=[smem] * 3 + [vmem] * 2,
        out_specs=[vmem, vmem, smem],
        cost_estimate=pl.CostEstimate(flops=flops, bytes_accessed=2_000_000, transcendentals=0),
        compiler_params=pltpu.CompilerParams(vmem_limit_bytes=48 * 1024 * 1024),
    )(source, dest, send_counts, features, vals)

    odd = list(range(rows - 1, 0, -2))
    even = list(range(rows - 2, -1, -2))
    *sent, turned = call(
        functools.partial(push_first_kernel, odd, tiles),
        [block] * len(odd) + [shape((span, width_in, size), BF16)],
        n_smem=2,
        n_vmem=cols + 1,
        flops=flops,
    )(place, code, own, *[far[k] for k in range(1, cols)], picked)
    kept = call(
        functools.partial(push_second_kernel, even),
        [block] * len(even),
        n_smem=2,
        n_vmem=2,
        flops=flops,
    )(place, code, turned, picked)

    summed = {k: [kept_k, send(sent_k, "rows", 1)] for k, kept_k, sent_k in zip(even, kept, sent)}
    bit = 2
    while bit < rows:
        for k in range(rows - bit, 0, -2 * bit):
            n = len(summed[k])
            both = call(add_kernel, block, n_vmem=n)(*summed.pop(k))
            summed[k ^ bit].append(send(both, "rows", bit))
        bit *= 2
    parts = summed[0]

    depth = width_in // 2
    part_shape = shape((depth + PAD, width), BF16)
    back, pre, part, away = call(
        functools.partial(middle_kernel, len(parts)),
        [shape((nodes, width_in), BF16), shape((nodes, width), F32), part_shape, part_shape],
        [pltpu.VMEM((width_in, width), F32)],
        1,
        len(parts) + 3,
        8 * width * width * nodes,
    )(place, *parts, weight, bias[None, :], cotangent)
    output = call(output_kernel, shape((nodes, width), BF16), n_vmem=1)(pre)

    part = call(add_kernel, part_shape, n_vmem=2)(part, send(away, "cols", 1))
    got = {0: back, 1: send(back, "rows", 1)}
    bit = 2
    while bit < cols:
        order = [got[1]]
        part = call(after_add_kernel, part_shape, n_vmem=2, n_any=len(order))(
            part, send(part, "cols", bit), *order
        )
        bit *= 2

    bit = rows // 2
    while bit > 1:
        for k in sorted(k for k in got if k % 2 == 0):
            got[k ^ bit] = send(got[k], "rows", bit)
        bit //= 2
    for k in range(2, rows - 2, 2):
        got[k + 1] = send(got[k], "rows", 1)

    got[rows - 1] = send(got[rows - 2], "rows", 1)
    first = [got[3]] if rows > 4 else []
    others = [got[k] for k in range(5, rows - 2, 2)]
    bit = rows // 2
    while bit > 1:
        order = others if bit == 2 else first
        part = call(after_add_kernel, part_shape, n_vmem=2, n_any=len(order))(
            part, send(part, "rows", bit), *order
        )
        bit //= 2
    after = part
    part = call(add_kernel, part_shape, n_vmem=2)(part, send(part, "rows", 1))
    half = part[:depth]
    other = send(half, "cols", 1)

    blocks = call(
        functools.partial(pull_kernel, rows, cols, tiles),
        [shape((nodes, width_in), BF16)] * cols,
        [pltpu.VMEM((span, size, width_in), F32)],
        2,
        rows + 1,
        flops,
        n_any=1,
    )(place, code, *[got[k] for k in range(rows)], picked, after)
    arrived = [blocks[0]]
    for k in range(cols - 2, 0, -2):
        near = send(blocks[k + 1], "cols", 1)
        both = call(add_kernel, shape((nodes, width_in), BF16), n_vmem=2)(blocks[k], near)
        arrived.append(send(both, "cols", k))
    arrived.append(send(blocks[1], "cols", 1))
    scale = 1.0 / math.sqrt(nodes * rows * cols)
    input_grad, weight_grad, bias_grad = call(
        functools.partial(last_kernel, len(arrived), scale),
        [
            shape((nodes, width_in), BF16),
            shape((width_in, width), F32),
            shape((1, width), F32),
        ],
        n_smem=1,
        n_vmem=len(arrived) + 2,
    )(place, *arrived, part, other)
    return output, input_grad, weight_grad, bias_grad[0]


def solution(mesh):
    in_specs = (
        P(("rows", "cols"), None),
        P(),
        P(),
        P("rows", "cols", None, None, None, None),
        P("rows", "cols", None, None),
        P("rows", "cols", None, None),
        P("rows", "cols", None),
        P(("rows", "cols"), None),
    )
    out_specs = (P(("rows", "cols"), None), P(("rows", "cols"), None), P(), P())
    return jax.shard_map(local, mesh=mesh, in_specs=in_specs, out_specs=out_specs, check_vma=False)
```

```python
import functools
import math

import jax
import jax.numpy as jnp
from jax import lax
from jax.experimental import pallas as pl
from jax.experimental.pallas import tpu as pltpu
from jax.sharding import PartitionSpec as P

F32 = jnp.float32
BF16 = jnp.bfloat16
PAD = 16


def call(body, out_shape, scratch=(), n_smem=0, n_vmem=0, flops=0, n_any=0):
    specs = [pl.BlockSpec(memory_space=pltpu.SMEM)] * n_smem
    specs += [pl.BlockSpec(memory_space=pltpu.VMEM)] * n_vmem
    specs += [pl.BlockSpec(memory_space=pl.ANY)] * n_any
    many = isinstance(out_shape, (list, tuple))
    vmem = pl.BlockSpec(memory_space=pltpu.VMEM)
    return pl.pallas_call(
        body,
        out_shape=out_shape,
        in_specs=specs,
        out_specs=[vmem] * len(out_shape) if many else vmem,
        scratch_shapes=list(scratch),
        cost_estimate=pl.CostEstimate(flops=flops, bytes_accessed=2_000_000, transcendentals=0),
        compiler_params=pltpu.CompilerParams(vmem_limit_bytes=48 * 1024 * 1024),
    )


def tree_sum(items):
    items = [x.astype(F32) for x in items]
    while len(items) > 1:
        items = [sum(items[i + 1 : i + 2], items[i]) for i in range(0, len(items), 2)]
    return items[0]


def send(x, axis, offset):
    size = lax.axis_size(axis)
    return lax.ppermute(x, axis, [(i, i ^ offset) for i in range(size)])


def prepare_kernel(
    tiles, source_ref, dest_ref, count_ref, feat_ref, vals_ref, picked_ref, own_ref, code_ref
):
    rows, slots, size, _ = vals_ref.shape
    for o in range(rows):
        for s in range(slots):
            code_ref[o * slots + s] = source_ref[0, s, 0, o]
    for k in range(tiles):
        own_ref[k] = feat_ref[k * size : (k + 1) * size, :].T
    for o in range(rows):
        for s in range(slots):
            live = s < count_ref[0, 0, o]
            dest = jnp.where(live, dest_ref[0, s, 0, o], tiles)
            block = vals_ref[o, s]
            zero = jnp.zeros_like(block)
            for t in range(tiles):
                picked_ref[o, s, :, t * size : (t + 1) * size] = jnp.where(dest == t, block, zero)


def push_one(k, place_ref, code_ref, turned, picked_ref):
    owner = place_ref[0] ^ k
    _, slots, size, wide = picked_ref.shape
    sources = jnp.concatenate([turned[code_ref[owner * slots + s]] for s in range(slots)], axis=1)
    chosen = picked_ref[owner].reshape(slots * size, wide)
    return jnp.dot(sources, chosen, preferred_element_type=F32).astype(BF16)


def push_first_kernel(ks, tiles, place_ref, code_ref, *refs):
    n = len(refs) - len(ks) - 1
    own_ref, far, picked_ref = refs[0], refs[1 : n - 1], refs[n - 1]
    outs, turned = refs[n:-1], refs[-1]
    size = picked_ref.shape[2]
    col = place_ref[1]
    for t in range(tiles):
        turned[col * tiles + t] = own_ref[t]
    for k, ref in enumerate(far, 1):
        for t in range(tiles):
            turned[(col ^ k) * tiles + t] = ref[t * size : (t + 1) * size, :].T
    for k, out_ref in zip(ks, outs):
        out_ref[...] = push_one(k, place_ref, code_ref, turned, picked_ref)


def push_second_kernel(ks, place_ref, code_ref, turned, picked_ref, *outs):
    for k, out_ref in zip(ks, outs):
        out_ref[...] = push_one(k, place_ref, code_ref, turned, picked_ref)


def add_kernel(*refs):
    refs[-1][...] = tree_sum([r[...] for r in refs[:-1]]).astype(refs[-1].dtype)


def middle_kernel(n_parts, place_ref, *refs):
    parts = refs[:n_parts]
    weight_ref, bias_ref, cot_ref, back_ref, pre_ref, keep_ref, away_ref, wg = refs[n_parts:]
    agg = tree_sum([p[...] for p in parts])
    high = agg.astype(BF16)
    low = (agg - high.astype(F32)).astype(BF16)
    dims = (((0,), (0,)), ((), ()))
    weight = weight_ref[...]
    pre = lax.dot_general(high, weight, dims, preferred_element_type=F32)
    pre += lax.dot_general(low, weight, dims, preferred_element_type=F32)
    pre += bias_ref[...]
    pre_ref[...] = pre
    c = math.sqrt(2.0 / math.pi)
    square = pre * pre
    t = jnp.tanh(c * pre * (1.0 + 0.044715 * square))
    slope = 0.5 * (1.0 + t) + 0.5 * pre * (1.0 - t * t) * (c * (1.0 + 3 * 0.044715 * square))
    grad = (cot_ref[...].astype(F32) * slope).astype(BF16)
    back_ref[...] = lax.dot_general(
        grad, weight, (((1,), (1,)), ((), ())), preferred_element_type=F32
    ).astype(BF16)
    wg[...] = jnp.dot(high, grad, preferred_element_type=F32)
    bias_row = jnp.sum(grad.astype(F32), axis=0, keepdims=True).astype(BF16)
    bias_rows = jnp.broadcast_to(bias_row, (PAD, bias_row.shape[1]))
    depth = wg.shape[0] // 2
    mine = place_ref[1] % 2
    for which, ref in ((mine, keep_ref), (1 - mine, away_ref)):
        ref[:depth, :] = wg[pl.ds(pl.multiple_of(which * depth, depth), depth), :].astype(BF16)
        ref[depth:, :] = bias_rows


def output_kernel(pre_ref, out_ref):
    pre = pre_ref[...]
    c = math.sqrt(2.0 / math.pi)
    t = jnp.tanh(c * pre * (1.0 + 0.044715 * pre * pre))
    out_ref[...] = (pre * (0.5 * (1.0 + t))).astype(BF16)


def after_add_kernel(a_ref, b_ref, *refs):
    refs[-1][...] = (a_ref[...].astype(F32) + b_ref[...].astype(F32)).astype(BF16)


def pull_kernel(rows, cols, tiles, place_ref, code_ref, *refs):
    grad_refs, picked_ref, outs, total = refs[:rows], refs[rows], refs[rows + 2 : -1], refs[-1]
    slots, size = picked_ref.shape[1], picked_ref.shape[2]
    row, col = place_ref[0], place_ref[1]
    total[...] = jnp.zeros_like(total)
    for k in range(rows):
        owner = row ^ k
        block = grad_refs[k][: tiles * size, :]
        terms = jnp.dot(
            picked_ref[owner].reshape(slots * size, block.shape[0]), block, preferred_element_type=F32
        )
        for s in range(slots):
            total[code_ref[owner * slots + s]] += terms[s * size : (s + 1) * size]
    for k in range(cols):
        for t in range(tiles):
            outs[k][t * size : (t + 1) * size, :] = total[(col ^ k) * tiles + t].astype(BF16)


def weight_kernel(scale, place_ref, part_ref, other_ref, wg_ref, bg_ref):
    depth = other_ref.shape[0]
    mine = place_ref[1] % 2
    for which, ref in ((mine, part_ref), (1 - mine, other_ref)):
        start = pl.multiple_of(which * depth, depth)
        wg_ref[pl.ds(start, depth), :] = ref[:depth, :].astype(F32) * scale
    bg_ref[...] = part_ref[depth : depth + 1, :].astype(F32) * scale


def local(features, weight, bias, tile_values, tile_source, tile_dest, send_counts, cotangent):
    rows, cols = lax.axis_size("rows"), lax.axis_size("cols")
    size = tile_values.shape[-1]
    slots = tile_values.shape[3]
    nodes, width_in = features.shape
    width = weight.shape[1]
    tiles = nodes // size
    span = tiles * cols
    vals = tile_values[0, 0]
    place = jnp.stack([lax.axis_index("rows"), lax.axis_index("cols")]).astype(jnp.int32)
    source = tile_source.transpose(0, 3, 1, 2)
    dest = tile_dest.transpose(0, 3, 1, 2)
    shape = jax.ShapeDtypeStruct
    block = shape((width_in, nodes), BF16)
    flops = rows * slots * size * size * tiles * width

    far = {k: send(features, "cols", k) for k in range(cols - 1, 0, -1)}
    smem, vmem = pl.BlockSpec(memory_space=pltpu.SMEM), pl.BlockSpec(memory_space=pltpu.VMEM)
    picked, own, code = pl.pallas_call(
        functools.partial(prepare_kernel, tiles),
        out_shape=[
            shape((rows, slots, size, tiles * size), BF16),
            shape((tiles, width_in, size), BF16),
            shape((rows * slots,), jnp.int32),
        ],
        in_specs=[smem] * 3 + [vmem] * 2,
        out_specs=[vmem, vmem, smem],
        cost_estimate=pl.CostEstimate(flops=flops, bytes_accessed=2_000_000, transcendentals=0),
        compiler_params=pltpu.CompilerParams(vmem_limit_bytes=48 * 1024 * 1024),
    )(source, dest, send_counts, features, vals)

    odd = list(range(rows - 1, 0, -2))
    even = list(range(rows - 2, -1, -2))
    *sent, turned = call(
        functools.partial(push_first_kernel, odd, tiles),
        [block] * len(odd) + [shape((span, width_in, size), BF16)],
        n_smem=2,
        n_vmem=cols + 1,
        flops=flops,
    )(place, code, own, *[far[k] for k in range(1, cols)], picked)
    kept = call(
        functools.partial(push_second_kernel, even),
        [block] * len(even),
        n_smem=2,
        n_vmem=2,
        flops=flops,
    )(place, code, turned, picked)

    summed = {k: [kept_k, send(sent_k, "rows", 1)] for k, kept_k, sent_k in zip(even, kept, sent)}
    bit = 2
    while bit < rows:
        for k in range(rows - bit, 0, -2 * bit):
            n = len(summed[k])
            both = call(add_kernel, block, n_vmem=n)(*summed.pop(k))
            summed[k ^ bit].append(send(both, "rows", bit))
        bit *= 2
    parts = summed[0]

    depth = width_in // 2
    part_shape = shape((depth + PAD, width), BF16)
    back, pre, part, away = call(
        functools.partial(middle_kernel, len(parts)),
        [shape((nodes, width_in), BF16), shape((nodes, width), F32), part_shape, part_shape],
        [pltpu.VMEM((width_in, width), F32)],
        1,
        len(parts) + 3,
        8 * width * width * nodes,
    )(place, *parts, weight, bias[None, :], cotangent)
    output = call(output_kernel, shape((nodes, width), BF16), n_vmem=1)(pre)

    part = call(add_kernel, part_shape, n_vmem=2)(part, send(away, "cols", 1))
    got = {0: back, 1: send(back, "rows", 1)}
    bit = 2
    while bit < cols:
        order = [got[1]]
        part = call(after_add_kernel, part_shape, n_vmem=2, n_any=len(order))(
            part, send(part, "cols", bit), *order
        )
        bit *= 2

    bit = rows // 2
    while bit > 1:
        for k in sorted(k for k in got if k % 2 == 0):
            got[k ^ bit] = send(got[k], "rows", bit)
        bit //= 2
    for k in range(2, rows - 2, 2):
        got[k + 1] = send(got[k], "rows", 1)

    got[rows - 1] = send(got[rows - 2], "rows", 1)
    first = [got[3]] if rows > 4 else []
    others = [got[k] for k in range(5, rows - 2, 2)]
    bit = rows // 2
    while bit > 1:
        order = others if bit == 2 else first
        part = call(after_add_kernel, part_shape, n_vmem=2, n_any=len(order))(
            part, send(part, "rows", bit), *order
        )
        bit //= 2
    after = part
    part = call(add_kernel, part_shape, n_vmem=2)(part, send(part, "rows", 1))
    half = part[:depth]
    other = send(half, "cols", 1)

    blocks = call(
        functools.partial(pull_kernel, rows, cols, tiles),
        [shape((nodes, width_in), BF16)] * cols,
        [pltpu.VMEM((span, size, width_in), F32)],
        2,
        rows + 1,
        flops,
        n_any=1,
    )(place, code, *[got[k] for k in range(rows)], picked, after)
    arrived = [blocks[0]]
    for k in range(cols - 2, 0, -2):
        near = send(blocks[k + 1], "cols", 1)
        both = call(add_kernel, shape((nodes, width_in), BF16), n_vmem=2)(blocks[k], near)
        arrived.append(send(both, "cols", k))
    arrived.append(send(blocks[1], "cols", 1))
    scale = 1.0 / math.sqrt(nodes * rows * cols)
    weight_grad, bias_grad = call(
        functools.partial(weight_kernel, scale),
        [shape((width_in, width), F32), shape((1, width), F32)],
        n_smem=1,
        n_vmem=2,
    )(place, part, other)
    input_grad = call(add_kernel, shape((nodes, width_in), BF16), n_vmem=len(arrived))(*arrived)
    return output, input_grad, weight_grad, bias_grad[0]


def solution(mesh):
    in_specs = (
        P(("rows", "cols"), None),
        P(),
        P(),
        P("rows", "cols", None, None, None, None),
        P("rows", "cols", None, None),
        P("rows", "cols", None, None),
        P("rows", "cols", None),
        P(("rows", "cols"), None),
    )
    out_specs = (P(("rows", "cols"), None), P(("rows", "cols"), None), P(), P())
    return jax.shard_map(local, mesh=mesh, in_specs=in_specs, out_specs=out_specs, check_vma=False)
```

```python
import functools
import math

import jax
import jax.numpy as jnp
from jax import lax
from jax.experimental import pallas as pl
from jax.experimental.pallas import tpu as pltpu
from jax.sharding import PartitionSpec as P

F32 = jnp.float32
BF16 = jnp.bfloat16
PAD = 16


def call(body, out_shape, scratch=(), n_smem=0, n_vmem=0, flops=0, n_any=0):
    specs = [pl.BlockSpec(memory_space=pltpu.SMEM)] * n_smem
    specs += [pl.BlockSpec(memory_space=pltpu.VMEM)] * n_vmem
    specs += [pl.BlockSpec(memory_space=pl.ANY)] * n_any
    many = isinstance(out_shape, (list, tuple))
    vmem = pl.BlockSpec(memory_space=pltpu.VMEM)
    return pl.pallas_call(
        body,
        out_shape=out_shape,
        in_specs=specs,
        out_specs=[vmem] * len(out_shape) if many else vmem,
        scratch_shapes=list(scratch),
        cost_estimate=pl.CostEstimate(flops=flops, bytes_accessed=2_000_000, transcendentals=0),
        compiler_params=pltpu.CompilerParams(vmem_limit_bytes=48 * 1024 * 1024),
    )


def tree_sum(items):
    items = [x.astype(F32) for x in items]
    while len(items) > 1:
        items = [sum(items[i + 1 : i + 2], items[i]) for i in range(0, len(items), 2)]
    return items[0]


def send(x, axis, offset):
    size = lax.axis_size(axis)
    return lax.ppermute(x, axis, [(i, i ^ offset) for i in range(size)])


def prepare_kernel(
    tiles, source_ref, dest_ref, count_ref, feat_ref, vals_ref, picked_ref, own_ref, code_ref
):
    rows, slots, size, _ = vals_ref.shape
    for o in range(rows):
        for s in range(slots):
            code_ref[o * slots + s] = source_ref[0, s, 0, o]
    for k in range(tiles):
        own_ref[k] = feat_ref[k * size : (k + 1) * size, :].T
    for o in range(rows):
        for s in range(slots):
            live = s < count_ref[0, 0, o]
            dest = jnp.where(live, dest_ref[0, s, 0, o], tiles)
            block = vals_ref[o, s]
            zero = jnp.zeros_like(block)
            for t in range(tiles):
                picked_ref[o, s, :, t * size : (t + 1) * size] = jnp.where(dest == t, block, zero)


def push_one(k, place_ref, code_ref, turned, picked_ref):
    owner = place_ref[0] ^ k
    _, slots, size, wide = picked_ref.shape
    sources = jnp.concatenate([turned[code_ref[owner * slots + s]] for s in range(slots)], axis=1)
    chosen = picked_ref[owner].reshape(slots * size, wide)
    return jnp.dot(sources, chosen, preferred_element_type=F32).astype(BF16)


def push_first_kernel(ks, tiles, place_ref, code_ref, *refs):
    n = len(refs) - len(ks) - 1
    own_ref, far, picked_ref = refs[0], refs[1 : n - 1], refs[n - 1]
    outs, turned = refs[n:-1], refs[-1]
    size = picked_ref.shape[2]
    col = place_ref[1]
    for t in range(tiles):
        turned[col * tiles + t] = own_ref[t]
    for k, ref in enumerate(far, 1):
        for t in range(tiles):
            turned[(col ^ k) * tiles + t] = ref[t * size : (t + 1) * size, :].T
    for k, out_ref in zip(ks, outs):
        out_ref[...] = push_one(k, place_ref, code_ref, turned, picked_ref)


def push_second_kernel(ks, place_ref, code_ref, turned, picked_ref, *outs):
    for k, out_ref in zip(ks, outs):
        out_ref[...] = push_one(k, place_ref, code_ref, turned, picked_ref)


def add_kernel(*refs):
    refs[-1][...] = tree_sum([r[...] for r in refs[:-1]]).astype(refs[-1].dtype)


def middle_kernel(n_parts, place_ref, *refs):
    parts = refs[:n_parts]
    weight_ref, bias_ref, cot_ref, back_ref, pre_ref, keep_ref, away_ref, wg = refs[n_parts:]
    agg = tree_sum([p[...] for p in parts])
    high = agg.astype(BF16)
    low = (agg - high.astype(F32)).astype(BF16)
    dims = (((0,), (0,)), ((), ()))
    weight = weight_ref[...]
    pre = lax.dot_general(high, weight, dims, preferred_element_type=F32)
    pre += lax.dot_general(low, weight, dims, preferred_element_type=F32)
    pre += bias_ref[...]
    pre_ref[...] = pre
    c = math.sqrt(2.0 / math.pi)
    square = pre * pre
    t = jnp.tanh(c * pre * (1.0 + 0.044715 * square))
    slope = 0.5 * (1.0 + t) + 0.5 * pre * (1.0 - t * t) * (c * (1.0 + 3 * 0.044715 * square))
    grad = (cot_ref[...].astype(F32) * slope).astype(BF16)
    back_ref[...] = lax.dot_general(
        grad, weight, (((1,), (1,)), ((), ())), preferred_element_type=F32
    ).astype(BF16)
    wg[...] = jnp.dot(high, grad, preferred_element_type=F32)
    bias_row = jnp.sum(grad.astype(F32), axis=0, keepdims=True).astype(BF16)
    bias_rows = jnp.broadcast_to(bias_row, (PAD, bias_row.shape[1]))
    depth = wg.shape[0] // 2
    mine = place_ref[1] % 2
    for which, ref in ((mine, keep_ref), (1 - mine, away_ref)):
        ref[:depth, :] = wg[pl.ds(pl.multiple_of(which * depth, depth), depth), :].astype(BF16)
        ref[depth:, :] = bias_rows


def output_kernel(pre_ref, out_ref):
    pre = pre_ref[...]
    c = math.sqrt(2.0 / math.pi)
    t = jnp.tanh(c * pre * (1.0 + 0.044715 * pre * pre))
    out_ref[...] = (pre * (0.5 * (1.0 + t))).astype(BF16)


def after_add_kernel(a_ref, b_ref, *refs):
    refs[-1][...] = (a_ref[...].astype(F32) + b_ref[...].astype(F32)).astype(BF16)


def pull_kernel(rows, cols, tiles, place_ref, code_ref, *refs):
    grad_refs, picked_ref, outs, total = refs[:rows], refs[rows], refs[rows + 2 : -1], refs[-1]
    slots, size = picked_ref.shape[1], picked_ref.shape[2]
    row, col = place_ref[0], place_ref[1]
    total[...] = jnp.zeros_like(total)
    for k in range(rows):
        owner = row ^ k
        block = grad_refs[k][: tiles * size, :]
        terms = jnp.dot(
            picked_ref[owner].reshape(slots * size, block.shape[0]), block, preferred_element_type=F32
        )
        for s in range(slots):
            total[code_ref[owner * slots + s]] += terms[s * size : (s + 1) * size]
    for k in range(cols):
        for t in range(tiles):
            outs[k][t * size : (t + 1) * size, :] = total[(col ^ k) * tiles + t].astype(BF16)


def weight_kernel(scale, place_ref, part_ref, other_ref, wg_ref, bg_ref):
    depth = other_ref.shape[0]
    mine = place_ref[1] % 2
    for which, ref in ((mine, part_ref), (1 - mine, other_ref)):
        start = pl.multiple_of(which * depth, depth)
        wg_ref[pl.ds(start, depth), :] = ref[:depth, :].astype(F32) * scale
    bg_ref[...] = part_ref[depth : depth + 1, :].astype(F32) * scale


def local(features, weight, bias, tile_values, tile_source, tile_dest, send_counts, cotangent):
    rows, cols = lax.axis_size("rows"), lax.axis_size("cols")
    size = tile_values.shape[-1]
    slots = tile_values.shape[3]
    nodes, width_in = features.shape
    width = weight.shape[1]
    tiles = nodes // size
    span = tiles * cols
    vals = tile_values[0, 0]
    place = jnp.stack([lax.axis_index("rows"), lax.axis_index("cols")]).astype(jnp.int32)
    source = tile_source.transpose(0, 3, 1, 2)
    dest = tile_dest.transpose(0, 3, 1, 2)
    shape = jax.ShapeDtypeStruct
    block = shape((width_in, nodes), BF16)
    flops = rows * slots * size * size * tiles * width

    far = {k: send(features, "cols", k) for k in range(cols - 1, 0, -1)}
    smem, vmem = pl.BlockSpec(memory_space=pltpu.SMEM), pl.BlockSpec(memory_space=pltpu.VMEM)
    picked, own, code = pl.pallas_call(
        functools.partial(prepare_kernel, tiles),
        out_shape=[
            shape((rows, slots, size, tiles * size), BF16),
            shape((tiles, width_in, size), BF16),
            shape((rows * slots,), jnp.int32),
        ],
        in_specs=[smem] * 3 + [vmem] * 2,
        out_specs=[vmem, vmem, smem],
        cost_estimate=pl.CostEstimate(flops=flops, bytes_accessed=2_000_000, transcendentals=0),
        compiler_params=pltpu.CompilerParams(vmem_limit_bytes=48 * 1024 * 1024),
    )(source, dest, send_counts, features, vals)

    odd = list(range(rows - 1, 0, -2))
    even = list(range(rows - 2, -1, -2))
    rest = [k for k in range(rows - 2, -1, -1)]
    first, turned = call(
        functools.partial(push_first_kernel, odd[:1], tiles),
        [block, shape((span, width_in, size), BF16)],
        n_smem=2,
        n_vmem=cols + 1,
        flops=flops,
    )(place, code, own, *[far[k] for k in range(1, cols)], picked)
    contrib = call(
        functools.partial(push_second_kernel, rest),
        [block] * len(rest),
        n_smem=2,
        n_vmem=2,
        flops=flops,
    )(place, code, turned, picked)

    contrib = dict(zip(rest, contrib))
    contrib[odd[0]] = first

    summed = {k: [contrib[k], send(contrib[k + 1], "rows", 1)] for k in even}
    bit = 2
    while bit < rows:
        for k in range(rows - bit, 0, -2 * bit):
            n = len(summed[k])
            both = call(add_kernel, block, n_vmem=n)(*summed.pop(k))
            summed[k ^ bit].append(send(both, "rows", bit))
        bit *= 2
    parts = summed[0]

    depth = width_in // 2
    part_shape = shape((depth + PAD, width), BF16)
    back, pre, part, away = call(
        functools.partial(middle_kernel, len(parts)),
        [shape((nodes, width_in), BF16), shape((nodes, width), F32), part_shape, part_shape],
        [pltpu.VMEM((width_in, width), F32)],
        1,
        len(parts) + 3,
        8 * width * width * nodes,
    )(place, *parts, weight, bias[None, :], cotangent)
    output = call(output_kernel, shape((nodes, width), BF16), n_vmem=1)(pre)

    part = call(add_kernel, part_shape, n_vmem=2)(part, send(away, "cols", 1))
    got = {0: back, 1: send(back, "rows", 1)}
    bit = 2
    while bit < cols:
        order = [got[1]]
        part = call(after_add_kernel, part_shape, n_vmem=2, n_any=len(order))(
            part, send(part, "cols", bit), *order
        )
        bit *= 2

    bit = rows // 2
    while bit > 1:
        for k in sorted(k for k in got if k % 2 == 0):
            got[k ^ bit] = send(got[k], "rows", bit)
        bit //= 2
    for k in range(2, rows - 2, 2):
        got[k + 1] = send(got[k], "rows", 1)

    got[rows - 1] = send(got[rows - 2], "rows", 1)
    first = [got[3]] if rows > 4 else []
    others = [got[k] for k in range(5, rows - 2, 2)]
    bit = rows // 2
    while bit > 1:
        order = others if bit == 2 else first
        part = call(after_add_kernel, part_shape, n_vmem=2, n_any=len(order))(
            part, send(part, "rows", bit), *order
        )
        bit //= 2
    after = part
    part = call(add_kernel, part_shape, n_vmem=2)(part, send(part, "rows", 1))
    half = part[:depth]
    other = send(half, "cols", 1)

    blocks = call(
        functools.partial(pull_kernel, rows, cols, tiles),
        [shape((nodes, width_in), BF16)] * cols,
        [pltpu.VMEM((span, size, width_in), F32)],
        2,
        rows + 1,
        flops,
        n_any=1,
    )(place, code, *[got[k] for k in range(rows)], picked, after)
    arrived = [blocks[0]]
    for k in range(cols - 2, 0, -2):
        near = send(blocks[k + 1], "cols", 1)
        both = call(add_kernel, shape((nodes, width_in), BF16), n_vmem=2)(blocks[k], near)
        arrived.append(send(both, "cols", k))
    arrived.append(send(blocks[1], "cols", 1))
    scale = 1.0 / math.sqrt(nodes * rows * cols)
    weight_grad, bias_grad = call(
        functools.partial(weight_kernel, scale),
        [shape((width_in, width), F32), shape((1, width), F32)],
        n_smem=1,
        n_vmem=2,
    )(place, part, other)
    input_grad = call(add_kernel, shape((nodes, width_in), BF16), n_vmem=len(arrived))(*arrived)
    return output, input_grad, weight_grad, bias_grad[0]


def solution(mesh):
    in_specs = (
        P(("rows", "cols"), None),
        P(),
        P(),
        P("rows", "cols", None, None, None, None),
        P("rows", "cols", None, None),
        P("rows", "cols", None, None),
        P("rows", "cols", None),
        P(("rows", "cols"), None),
    )
    out_specs = (P(("rows", "cols"), None), P(("rows", "cols"), None), P(), P())
    return jax.shard_map(local, mesh=mesh, in_specs=in_specs, out_specs=out_specs, check_vma=False)
```
